32 devices in a mesh: req: 4 (over y, core), head: 2 (over x), blk: 4 (over z).
Axes of the slice: x: 2, y: 2, z: 4, core: 2. Of those that a mesh axis runs over, the one named last changes fastest.
Arguments:
- image_hidden: bfloat16 [16, 32, 32, 1536], P('req', 'head', 'blk'), parts along dimension 0, may hold values from -6 to 6
- text_hidden: bfloat16 [16, 160, 1536], P('req', ('head', 'blk')), parts along dimension 0, may hold values from -6 to 6
- latent_grid: float32 [16, 64, 64, 16], P('req', 'head', 'blk'), parts along dimension 0, may hold values from -6 to 6
- text_lengths: int32 [16], P('req'), parts along dimension 0, may hold values from 38 to 154, as said below
- step_index: int32 [16], P('req'), parts along dimension 0, may hold values from 125 to 999
- image_mod: float32 [16, 6, 1536], P('req'), parts along dimension 0, may hold values from -3 to 3
- text_mod: float32 [16, 6, 1536], P('req'), parts along dimension 0, may hold values from -3 to 3
- final_mod: float32 [16, 2, 1536], P('req'), parts along dimension 0, may hold values from -3 to 3
- image_qk_gain: float32 [2, 64], replicated, may hold values from 0.5 to 2.3
- text_qk_gain: float32 [2, 64], replicated, may hold values from 0.5 to 2.3
- image_qkv: bfloat16 [1536, 3, 1536], P(None, None, 'head'), may hold values from -0.15625 to 0.15625
- text_qkv: bfloat16 [1536, 3, 1536], P(None, None, 'head'), may hold values from -0.15625 to 0.15625
- image_proj: bfloat16 [1536, 1536], P('head'), may hold values from -0.15625 to 0.15625
- text_proj: bfloat16 [1536, 1536], P('head'), may hold values from -0.15625 to 0.15625
- image_up: bfloat16 [1536, 6144], P(None, 'head'), may hold values from -0.15625 to 0.15625
- text_up: bfloat16 [1536, 6144], P(None, 'head'), may hold values from -0.15625 to 0.15625
- image_down: bfloat16 [6144, 1536], P('head'), may hold values from -0.078125 to 0.078125
- text_down: bfloat16 [6144, 1536], P('head'), may hold values from -0.078125 to 0.078125
- final_proj: bfloat16 [1536, 64], replicated, may hold values from -0.15625 to 0.15625
- conv_kernel: bfloat16 [3, 3, 16, 512], replicated, may hold values from -0.5 to 0.5
Outputs:
- image_states: bfloat16 [16, 32, 32, 1536], P('req', 'head', 'blk'), parts along dimension 0
- text_states: bfloat16 [16, 160, 1536], P('req', ('head', 'blk')), parts along dimension 0
- latent_next: float32 [16, 64, 64, 16], P('req', 'head', 'blk'), parts along dimension 0
- features: bfloat16 [16, 64, 64, 512], P('req', 'head', 'blk'), parts along dimension 0
The draws below stay inside these ranges and needn't reach their ends.
There are 4 independent parts, one for each index of `req`. The reference program is written for one: setup_inputs(seed, part) draws one part's arguments, and reference() takes and returns one part's arrays. A program takes and returns all parts, laid end to end along the dimension named above; an argument that names none is the same for every part. Nothing has to cross between parts.
Inputs may be any that keep to these rules, and one draw needn't show every extreme that they name: `text_lengths`: every request has 154 or fewer live text tokens, and in each group one request has exactly 154.
All inputs are finite; a program needn't handle non-finite values.
Results may differ from the reference program's by a relative error of at most 0.012.
Values may be sent and summed in bfloat16 or wider, within the bound.
A program may use at most 192 MiB of HBM per device.

```python
import jax
import jax.numpy as jnp
from jax import lax

D = 1536
HEADS = 24
HD = 64
FF = 6144
LC = 16
CONV = 512
PC = 64
GRID = 32
TXT = 160
TXT_MAX = 154
REQ = 4


def draw_text_lengths(key, part):
    first_key, second_key = jax.random.split(jax.random.fold_in(key, 17))
    drawn = jax.random.randint(first_key, (REQ,), TXT_MAX // 4, TXT_MAX + 1)
    chosen = jax.random.randint(second_key, (), 0, REQ)
    return jnp.where(jnp.arange(REQ) == chosen, TXT_MAX, drawn).astype(jnp.int32)


def touch_ends(values, rng, smallest, top_value):
    longest = values.shape.index(max(values.shape))
    spots = []
    for shift in (0, 1):
        where = [jax.random.randint(jax.random.fold_in(rng, axis), (), 0, length) for axis, length in enumerate(values.shape)]
        where[longest] = (where[longest] + shift) % values.shape[longest]
        spots.append(tuple(where))
    return values.at[spots[0]].set(smallest).at[spots[1]].set(top_value)


def block_levels(own_key, extent, shards, smallest, largest):
    def one(dim, blocks):
        steps = jax.random.uniform(jax.random.fold_in(jax.random.fold_in(own_key, 6), dim), (blocks,), jnp.float32, smallest / len(shards), largest / len(shards))
        return jnp.repeat(jnp.exp(steps), extent[dim] // blocks).reshape((-1,) + (1,) * (len(extent) - dim - 1))

    level = one(*shards[0])
    for cut in shards[1:]:
        level = level * one(*cut)
    return level


def bell_draw(own_key, dims, scale, most, cuts=(), held_as=jnp.bfloat16):
    values = scale * jax.random.normal(own_key, dims, jnp.float32)
    if cuts:
        values = values * block_levels(own_key, dims, cuts, -0.22, 0.18)
    return jnp.clip(values, -most, most).astype(held_as)


def setup_inputs(seed: int = 0, part: int = 0) -> dict:
    splits = jax.random.split(jax.random.key(seed), 21)
    part_splits = jax.random.split(jax.random.fold_in(splits[20], part), 21)
    return {
        "image_hidden": bell_draw(part_splits[0], (REQ, GRID, GRID, D), 1.0, 6.0, ((1, 2), (2, 4))),
        "text_hidden": bell_draw(part_splits[1], (REQ, TXT, D), 1.0, 6.0, ((1, 8),)),
        "latent_grid": bell_draw(part_splits[2], (REQ, 2 * GRID, 2 * GRID, LC), 1.0, 6.0, ((1, 2), (2, 4)), jnp.float32),
        "text_lengths": draw_text_lengths(jax.random.fold_in(jax.random.fold_in(splits[20], part), 71), part),
        "step_index": touch_ends(jax.random.randint(part_splits[4], (REQ,), 125, 1000), jax.random.fold_in(part_splits[4], 1), 125, 999).astype(jnp.int32),
        "image_mod": bell_draw(part_splits[5], (REQ, 6, D), 0.5, 3.0, (), jnp.float32),
        "text_mod": bell_draw(part_splits[6], (REQ, 6, D), 0.5, 3.0, (), jnp.float32),
        "final_mod": bell_draw(part_splits[7], (REQ, 2, D), 0.5, 3.0, (), jnp.float32),
        "image_qk_gain": jnp.clip(jax.random.uniform(splits[8], (2, HD), jnp.float32, 0.5, 2.3), 0.5, 2.3),
        "text_qk_gain": jnp.clip(jax.random.uniform(splits[9], (2, HD), jnp.float32, 0.5, 2.3), 0.5, 2.3),
        "image_qkv": bell_draw(splits[10], (D, 3, HEADS * HD), D ** -0.5, 0.15625, ((2, 2),)),
        "text_qkv": bell_draw(splits[11], (D, 3, HEADS * HD), D ** -0.5, 0.15625, ((2, 2),)),
        "image_proj": bell_draw(splits[12], (HEADS * HD, D), D ** -0.5, 0.15625, ((0, 2),)),
        "text_proj": bell_draw(splits[13], (HEADS * HD, D), D ** -0.5, 0.15625, ((0, 2),)),
        "image_up": bell_draw(splits[14], (D, FF), D ** -0.5, 0.15625, ((1, 2),)),
        "text_up": bell_draw(splits[15], (D, FF), D ** -0.5, 0.15625, ((1, 2),)),
        "image_down": bell_draw(splits[16], (FF, D), FF ** -0.5, 0.078125, ((0, 2),)),
        "text_down": bell_draw(splits[17], (FF, D), FF ** -0.5, 0.078125, ((0, 2),)),
        "final_proj": bell_draw(splits[18], (D, PC), D ** -0.5, 0.15625),
        "conv_kernel": bell_draw(splits[19], (3, 3, LC, CONV), (9 * LC) ** -0.5, 0.5),
    }


def widen(values):
    return lax.optimization_barrier(values.astype(jnp.bfloat16)).astype(jnp.float32)

def expand(vector, values):
    return vector.reshape((vector.shape[0],) + (1,) * (values.ndim - 2) + (vector.shape[-1],))

def modulate(values, shift, scale):
    average = lax.optimization_barrier(jnp.mean(values, -1, keepdims=True))
    centred = values - average
    spread = lax.optimization_barrier(jnp.mean(centred * centred, -1, keepdims=True))
    normed = centred * lax.rsqrt(spread + 1e-06)
    return normed * (1.0 + expand(scale, values)) + expand(shift, values)

def head_norm(values, gain):
    shaped = values.reshape(values.shape[:-1] + (HEADS, HD))
    return widen(shaped * lax.rsqrt(lax.optimization_barrier(jnp.mean(shaped * shaped, -1, keepdims=True)) + 1e-06) * gain)

def noise_level(fraction):
    return 3.0 * fraction / (1.0 + 2.0 * fraction)

def attention_inputs(normed, weight, gains):
    projected = jnp.einsum('rnd,dje->rnje', normed, weight.astype(jnp.float32))
    queries = head_norm(projected[:, :, 0], gains[0])
    key_heads = head_norm(projected[:, :, 1], gains[1])
    value_heads = widen(projected[:, :, 2].reshape(queries.shape))
    return (queries, key_heads, value_heads)

def reference(image_hidden, text_hidden, latent_grid, text_lengths, step_index, image_mod, text_mod, final_mod, image_qk_gain, text_qk_gain, image_qkv, text_qkv, image_proj, text_proj, image_up, text_up, image_down, text_down, final_proj, conv_kernel):
    image_rows = GRID * GRID
    image_flat = image_hidden.astype(jnp.float32).reshape(REQ, image_rows, D)
    text_flat = text_hidden.astype(jnp.float32)
    image_norm = widen(modulate(image_flat, image_mod[:, 0], image_mod[:, 1]))
    text_norm = widen(modulate(text_flat, text_mod[:, 0], text_mod[:, 1]))
    image_q, image_k, image_v = attention_inputs(image_norm, image_qkv, image_qk_gain)
    text_q, text_k, text_v = attention_inputs(text_norm, text_qkv, text_qk_gain)
    queries = jnp.concatenate([image_q, text_q], 1)
    key_heads = jnp.concatenate([image_k, text_k], 1)
    value_heads = jnp.concatenate([image_v, text_v], 1)
    slot_ids = jnp.arange(TXT, dtype=jnp.int32)
    score_scale = 1.0 / HD ** 0.5

    def attend_one(items):
        query_one, key_one, value_one, length = items
        usable = jnp.concatenate([jnp.ones((image_rows,), jnp.float32), (slot_ids < length).astype(jnp.float32)])
        scores = jnp.einsum('qhd,khd->hqk', query_one, key_one) * score_scale
        weights = jnp.exp(scores) * usable[None, None, :]
        denominator = lax.optimization_barrier(jnp.sum(weights, -1))
        numerator = jnp.einsum('hqk,khd->hqd', widen(weights), value_one)
        context = (numerator / denominator[:, :, None]).astype(jnp.bfloat16)
        return context.transpose(1, 0, 2).reshape(image_rows + TXT, HEADS * HD)
    context = lax.map(attend_one, (queries, key_heads, value_heads, text_lengths))
    context = widen(context)
    image_attn = jnp.einsum('rne,ed->rnd', context[:, :image_rows], image_proj.astype(jnp.float32))
    text_attn = jnp.einsum('rne,ed->rnd', context[:, image_rows:], text_proj.astype(jnp.float32))
    image_mid = image_flat + expand(image_mod[:, 2], image_attn) * image_attn
    text_mid = text_flat + expand(text_mod[:, 2], text_attn) * text_attn
    image_in = widen(modulate(image_mid, image_mod[:, 3], image_mod[:, 4]))
    text_in = widen(modulate(text_mid, text_mod[:, 3], text_mod[:, 4]))
    image_hid = widen(jax.nn.gelu(jnp.einsum('rnd,df->rnf', image_in, image_up.astype(jnp.float32)), approximate=True))
    text_hid = widen(jax.nn.gelu(jnp.einsum('rnd,df->rnf', text_in, text_up.astype(jnp.float32)), approximate=True))
    image_back = jnp.einsum('rnf,fd->rnd', image_hid, image_down.astype(jnp.float32))
    text_back = jnp.einsum('rnf,fd->rnd', text_hid, text_down.astype(jnp.float32))
    image_out = image_mid + expand(image_mod[:, 5], image_back) * image_back
    image_states = image_out.reshape(REQ, GRID, GRID, D).astype(jnp.bfloat16)
    text_states = (text_mid + expand(text_mod[:, 5], text_back) * text_back).astype(jnp.bfloat16)
    final_in = widen(modulate(image_out, final_mod[:, 1], final_mod[:, 0]))
    velocity = jnp.einsum('rnd,dp->rnp', final_in, final_proj.astype(jnp.float32))
    velocity = velocity.reshape(REQ, GRID, GRID, 2, 2, LC).transpose(0, 1, 3, 2, 4, 5).reshape(REQ, 2 * GRID, 2 * GRID, LC)
    current = step_index.astype(jnp.float32) / 1000.0
    following = jnp.maximum(step_index - 125, 0).astype(jnp.float32) / 1000.0
    step_size = noise_level(following) - noise_level(current)
    latent_next = latent_grid + step_size[:, None, None, None] * velocity
    decoded_in = widen(latent_next / 1.5305 + 0.0609)
    padded = jnp.pad(decoded_in, ((0, 0), (1, 1), (1, 1), (0, 0)))
    out_rows = 2 * GRID
    summed = jnp.zeros((REQ, out_rows, out_rows, CONV), jnp.float32)
    kernel_wide = conv_kernel.astype(jnp.float32)
    for row_off in range(3):
        for col_off in range(3):
            summed = summed + jnp.einsum('rhwc,co->rhwo', padded[:, row_off:row_off + out_rows, col_off:col_off + out_rows], kernel_wide[row_off, col_off])
    return (image_states, text_states, latent_next, summed.astype(jnp.bfloat16))
```

```python
import functools

import jax
import jax.numpy as jnp
from jax import lax
from jax.experimental import pallas as pl
from jax.experimental.pallas import tpu as pltpu
from jax.sharding import PartitionSpec as P

HD = 64
CHUNKS = 1


def modulate(values, shift, scale):
    average = jnp.mean(values, -1, keepdims=True)
    centred = values - average
    spread = jnp.mean(centred * centred, -1, keepdims=True)
    normed = centred * lax.rsqrt(spread + 1e-06)
    return normed * (1.0 + scale[:, None, :]) + shift[:, None, :]


def noise_level(fraction):
    return 3.0 * fraction / (1.0 + 2.0 * fraction)


def dot(values, weight):
    return jnp.einsum("rnd,df->rnf", values, weight, preferred_element_type=jnp.float32)


def normed_heads(values, gain):
    return values * lax.rsqrt(jnp.mean(values * values, -1, keepdims=True) + 1e-06) * gain


def attention_kernel(parts, heads, step, *refs):
    count = parts + 1
    q_refs, k_refs, v_refs = refs[:count], refs[count : 2 * count], refs[2 * count : 3 * count]
    image_gain, text_gain, usable = refs[3 * count : 3 * count + 3]
    o_refs = refs[3 * count + 3 : 4 * count + 3]
    keys, vals = refs[4 * count + 3 :]
    for head in range(heads):
        lanes = slice(head * HD, (head + 1) * HD)
        start = 0
        for part in range(count):
            rows = k_refs[part].shape[1]
            gain = (image_gain if part < parts else text_gain)[1:2, :]
            keys[start : start + rows, :] = normed_heads(k_refs[part][0, :, lanes], gain).astype(
                jnp.bfloat16
            )
            value = v_refs[part][0, :, lanes].astype(jnp.float32)
            if part < parts:
                ones = jnp.ones((rows, HD), jnp.float32)
            else:
                mask = usable[0]
                value = value * mask
                ones = jnp.broadcast_to(mask, (rows, HD))
            vals[start : start + rows, :] = jnp.concatenate([value, ones], 1).astype(jnp.bfloat16)
            start += rows
        for part in range(count):
            rows = q_refs[part].shape[1]
            gain = (image_gain if part < parts else text_gain)[0:1, :]
            size = step if rows % step == 0 else rows
            for low in range(0, rows, size):
                query = normed_heads(q_refs[part][0, low : low + size, lanes], gain)
                query = query.astype(jnp.bfloat16) * 0.125
                scores = lax.dot_general(
                    query, keys[...], (((1,), (1,)), ((), ())), preferred_element_type=jnp.float32
                )
                weights = jnp.exp(scores).astype(jnp.bfloat16)
                total = jnp.dot(weights, vals[...], preferred_element_type=jnp.float32)
                o_refs[part][0, low : low + size, lanes] = (
                    total[:, :HD] / total[:, HD : HD + 1]
                ).astype(jnp.bfloat16)


def attend(queries, keys, values, image_gain, text_gain, usable):
    parts = len(queries) - 1
    requests, _, width = queries[0].shape
    heads = width // HD
    group = 2 if heads % 2 == 0 else heads

    def spec(array):
        return pl.BlockSpec((1, array.shape[1], group * HD), lambda r, g: (r, 0, g))

    whole = pl.BlockSpec((2, HD), lambda r, g: (0, 0))
    total_keys = sum(a.shape[1] for a in keys)
    total_queries = sum(a.shape[1] for a in queries)
    return pl.pallas_call(
        functools.partial(attention_kernel, parts, group, 256),
        grid=(requests, heads // group),
        in_specs=[spec(a) for a in (*queries, *keys, *values)]
        + [whole, whole, pl.BlockSpec((1,) + usable.shape[1:], lambda r, g: (r, 0, 0))],
        out_specs=[spec(a) for a in queries],
        out_shape=[jax.ShapeDtypeStruct(a.shape, jnp.bfloat16) for a in queries],
        scratch_shapes=[
            pltpu.VMEM((total_keys, HD), jnp.bfloat16),
            pltpu.VMEM((total_keys, 2 * HD), jnp.bfloat16),
        ],
        compiler_params=pltpu.CompilerParams(vmem_limit_bytes=40 * 2**20),
        cost_estimate=pl.CostEstimate(
            flops=16 * requests * heads * total_queries * total_keys * HD,
            bytes_accessed=requests * width * (total_keys * 6 + total_queries * 6),
            transcendentals=requests * heads * total_queries * total_keys,
        ),
    )(*queries, *keys, *values, image_gain, text_gain, usable)


def extended(block, sides, width):
    for axis, dim in sides:
        count = lax.axis_size(axis)
        forward = [(i, i + 1) for i in range(count - 1)]
        backward = [(target, source) for source, target in forward]
        low = lax.ppermute(
            lax.slice_in_dim(block, block.shape[dim] - width, None, axis=dim), axis, forward
        )
        high = lax.ppermute(lax.slice_in_dim(block, 0, width, axis=dim), axis, backward)
        block = jnp.concatenate([low, block, high], axis=dim)
    return block


def convolve(padded, kernel):
    out_rows = padded.shape[1] - 2
    out_cols = padded.shape[2] - 2
    patches = jnp.concatenate(
        [
            padded[:, row : row + out_rows, col : col + out_cols]
            for row in range(3)
            for col in range(3)
        ],
        -1,
    )
    flat = kernel.reshape(-1, kernel.shape[-1])
    return jnp.einsum(
        "rhwc,co->rhwo", patches, flat, preferred_element_type=jnp.float32
    ).astype(jnp.bfloat16)


def body(
    image_hidden,
    text_hidden,
    latent_grid,
    text_lengths,
    step_index,
    image_mod,
    text_mod,
    final_mod,
    image_qk_gain,
    text_qk_gain,
    image_qkv,
    text_qkv,
    image_proj,
    text_proj,
    image_up,
    text_up,
    image_down,
    text_down,
    final_proj,
    conv_kernel,
):
    heads, blocks = lax.axis_size("head"), lax.axis_size("blk")
    my_head, my_blk = lax.axis_index("head"), lax.axis_index("blk")
    requests, tile_rows, tile_cols, model = image_hidden.shape
    slots = text_hidden.shape[1]
    mine = requests // blocks
    patches = tile_rows * tile_cols

    def of_block(array, block):
        return lax.dynamic_slice_in_dim(array, block * mine, mine, axis=0)

    def scatter(array):
        pieces = [of_block(array, my_blk)]
        for off in range(1, blocks):
            perm = [(i, (i + off) % blocks) for i in range(blocks)]
            pieces.append(lax.ppermute(of_block(array, (my_blk + off) % blocks), "blk", perm))
        return pieces

    def collect(pieces):
        held = [pieces[0]]
        for off in range(1, blocks):
            perm = [(i, (i - off) % blocks) for i in range(blocks)]
            held.append(lax.ppermute(pieces[off], "blk", perm))
        joined = jnp.concatenate(held, 0)
        return jnp.roll(joined, my_blk * mine, axis=0)

    def fetch(array, off):
        return lax.ppermute(array, "head", [(i, (i - off) % heads) for i in range(heads)])

    def give(array, off):
        return lax.ppermute(array, "head", [(i, (i + off) % heads) for i in range(heads)])

    image_m, text_m, final_m = (of_block(a, my_blk) for a in (image_mod, text_mod, final_mod))
    lengths = of_block(text_lengths, my_blk)

    text_x = scatter(text_hidden)
    image_x = scatter(image_hidden.reshape(requests, patches, model))
    text_x = jnp.concatenate(text_x, 1).astype(jnp.float32)
    text_a = modulate(text_x, text_m[:, 0], text_m[:, 1]).astype(jnp.bfloat16)
    text_all = jnp.concatenate([text_a] + [fetch(text_a, off) for off in range(1, heads)], 1)
    image_x = [piece.astype(jnp.float32) for piece in image_x]
    image_a = [
        modulate(piece, image_m[:, 0], image_m[:, 1]).astype(jnp.bfloat16) for piece in image_x
    ]
    parts = [jnp.concatenate(image_a, 1)]
    for off in range(1, heads):
        parts.append(jnp.concatenate([fetch(piece, off) for piece in image_a], 1))

    position = jnp.arange(heads * blocks * slots, dtype=jnp.int32)
    head_off = position // (blocks * slots)
    blk_off = (position // slots) % blocks
    owner = ((my_head + head_off) % heads) * blocks + (my_blk - blk_off) % blocks
    slot_ids = owner * slots + position % slots
    usable = (slot_ids[None, :] < lengths[:, None]).astype(jnp.float32)[:, :, None]

    queries, keys, values = [], [], []
    for tokens, weight in [(part, image_qkv) for part in parts] + [(text_all, text_qkv)]:
        queries.append(dot(tokens, weight[:, 0]))
        keys.append(dot(tokens, weight[:, 1]))
        values.append(dot(tokens, weight[:, 2]).astype(jnp.bfloat16))
    contexts = attend(queries, keys, values, image_qk_gain, text_qk_gain, usable)

    def layer(hidden, parts, mod, proj, up, down):
        total = None
        for off in range(heads - 1, -1, -1):
            share = dot(parts[off], proj)
            if off:
                share = give(share.astype(jnp.bfloat16), off).astype(jnp.float32)
            total = share if total is None else total + share
        mid = hidden + mod[:, 2][:, None, :] * total
        local = modulate(mid, mod[:, 3], mod[:, 4]).astype(jnp.bfloat16)
        total = None
        for off in range(heads - 1, -1, -1):
            tokens = fetch(local, off) if off else local
            hid = jax.nn.gelu(dot(tokens, up), approximate=True).astype(jnp.bfloat16)
            share = dot(hid, down)
            if off:
                share = give(share.astype(jnp.bfloat16), off).astype(jnp.float32)
            total = share if total is None else total + share
        return mid + mod[:, 5][:, None, :] * total

    share = blocks * slots
    text_parts = [contexts[-1][:, off * share : (off + 1) * share] for off in range(heads)]
    text_y = layer(text_x, text_parts, text_m, text_proj, text_up, text_down).astype(jnp.bfloat16)

    state_pieces, velocity_pieces = [], []
    per = blocks // CHUNKS
    for chunk in range(CHUNKS):
        low, high = chunk * per * patches, (chunk + 1) * per * patches
        image_y = layer(
            jnp.concatenate(image_x[chunk * per : (chunk + 1) * per], 1),
            [context[:, low:high] for context in contexts[:-1]],
            image_m,
            image_proj,
            image_up,
            image_down,
        )
        final_in = modulate(image_y, final_m[:, 1], final_m[:, 0]).astype(jnp.bfloat16)
        velocity = dot(final_in, final_proj)
        for piece in range(per):
            rows = slice(piece * patches, (piece + 1) * patches)
            velocity_pieces.append(velocity[:, rows])
            state_pieces.append(image_y[:, rows].astype(jnp.bfloat16))

    velocity = collect(velocity_pieces)
    image_states = collect(state_pieces).reshape(image_hidden.shape)
    text_states = collect([text_y[:, i * slots : (i + 1) * slots] for i in range(blocks)])

    channels = velocity.shape[-1] // 4
    velocity = (
        velocity.reshape(requests, tile_rows, tile_cols, 2, 2, channels)
        .transpose(0, 1, 3, 2, 4, 5)
        .reshape(requests, 2 * tile_rows, 2 * tile_cols, channels)
    )
    current = step_index.astype(jnp.float32) / 1000.0
    following = jnp.maximum(step_index - 125, 0).astype(jnp.float32) / 1000.0
    step_size = noise_level(following) - noise_level(current)
    latent_next = latent_grid + step_size[:, None, None, None] * velocity
    decoded_in = (latent_next / 1.5305 + 0.0609).astype(jnp.bfloat16)
    padded = extended(decoded_in, (("head", 1), ("blk", 2)), 1)
    features = convolve(padded, conv_kernel)
    return (image_states, text_states, latent_next, features)


def solution(mesh):
    in_specs = (
        P("req", "head", "blk", None),
        P("req", ("head", "blk"), None),
        P("req", "head", "blk", None),
        P("req"),
        P("req"),
        P("req", None, None),
        P("req", None, None),
        P("req", None, None),
        P(),
        P(),
        P(None, None, "head"),
        P(None, None, "head"),
        P("head", None),
        P("head", None),
        P(None, "head"),
        P(None, "head"),
        P("head", None),
        P("head", None),
        P(),
        P(),
    )
    out_specs = (
        P("req", "head", "blk", None),
        P("req", ("head", "blk"), None),
        P("req", "head", "blk", None),
        P("req", "head", "blk", None),
    )
    return jax.shard_map(body, mesh=mesh, in_specs=in_specs, out_specs=out_specs, check_vma=False)
```

```python
import functools

import jax
import jax.numpy as jnp
from jax import lax
from jax.experimental import pallas as pl
from jax.experimental.pallas import tpu as pltpu
from jax.sharding import PartitionSpec as P

HD = 64
apart = lax.optimization_barrier
CHUNKS = 2


def modulate(values, shift, scale):
    average = jnp.mean(values, -1, keepdims=True)
    centred = values - average
    spread = jnp.mean(centred * centred, -1, keepdims=True)
    normed = centred * lax.rsqrt(spread + 1e-06)
    return normed * (1.0 + scale[:, None, :]) + shift[:, None, :]


def noise_level(fraction):
    return 3.0 * fraction / (1.0 + 2.0 * fraction)


def dot(values, weight):
    return jnp.einsum("rnd,df->rnf", values, weight, preferred_element_type=jnp.float32)


def normed_heads(values, gain):
    return values * lax.rsqrt(jnp.mean(values * values, -1, keepdims=True) + 1e-06) * gain


def attention_kernel(parts, asked, text_at, heads, step, *refs):
    count = parts + 1
    q_refs, refs = refs[:asked], refs[asked:]
    k_refs, v_refs, refs = refs[:count], refs[count : 2 * count], refs[2 * count :]
    image_gain, text_gain, usable = refs[:3]
    o_refs = refs[3 : 3 + asked]
    keys, vals = refs[3 + asked :]
    for head in range(heads):
        lanes = slice(head * HD, (head + 1) * HD)
        start = 0
        for part in range(count):
            rows = k_refs[part].shape[1]
            gain = (image_gain if part < parts else text_gain)[1:2, :]
            keys[start : start + rows, :] = normed_heads(k_refs[part][0, :, lanes], gain).astype(
                jnp.bfloat16
            )
            value = v_refs[part][0, :, lanes].astype(jnp.float32)
            if part < parts:
                ones = jnp.ones((rows, HD), jnp.float32)
            else:
                mask = usable[0]
                value = value * mask
                ones = jnp.broadcast_to(mask, (rows, HD))
            vals[start : start + rows, :] = jnp.concatenate([value, ones], 1).astype(jnp.bfloat16)
            start += rows
        for part in range(asked):
            rows = q_refs[part].shape[1]
            gain = (text_gain if part == text_at else image_gain)[0:1, :]
            size = step if rows % step == 0 else rows
            for low in range(0, rows, size):
                query = normed_heads(q_refs[part][0, low : low + size, lanes], gain)
                query = query.astype(jnp.bfloat16) * 0.125
                scores = lax.dot_general(
                    query, keys[...], (((1,), (1,)), ((), ())), preferred_element_type=jnp.float32
                )
                weights = jnp.exp(scores).astype(jnp.bfloat16)
                total = jnp.dot(weights, vals[...], preferred_element_type=jnp.float32)
                o_refs[part][0, low : low + size, lanes] = (
                    total[:, :HD] / total[:, HD : HD + 1]
                ).astype(jnp.bfloat16)


def attend(queries, text_at, keys, values, image_gain, text_gain, usable):
    parts = len(keys) - 1
    requests, _, width = queries[0].shape
    heads = width // HD
    group = 2 if heads % 2 == 0 else heads

    def spec(array):
        return pl.BlockSpec((1, array.shape[1], group * HD), lambda r, g: (r, 0, g))

    whole = pl.BlockSpec((2, HD), lambda r, g: (0, 0))
    total_keys = sum(a.shape[1] for a in keys)
    total_queries = sum(a.shape[1] for a in queries)
    return pl.pallas_call(
        functools.partial(attention_kernel, parts, len(queries), text_at, group, 256),
        grid=(requests, heads // group),
        in_specs=[spec(a) for a in (*queries, *keys, *values)]
        + [whole, whole, pl.BlockSpec((1,) + usable.shape[1:], lambda r, g: (r, 0, 0))],
        out_specs=[spec(a) for a in queries],
        out_shape=[jax.ShapeDtypeStruct(a.shape, jnp.bfloat16) for a in queries],
        scratch_shapes=[
            pltpu.VMEM((total_keys, HD), jnp.bfloat16),
            pltpu.VMEM((total_keys, 2 * HD), jnp.bfloat16),
        ],
        compiler_params=pltpu.CompilerParams(vmem_limit_bytes=40 * 2**20),
        cost_estimate=pl.CostEstimate(
            flops=16 * requests * heads * total_queries * total_keys * HD,
            bytes_accessed=requests * width * (total_keys * 6 + total_queries * 6),
            transcendentals=requests * heads * total_queries * total_keys,
        ),
    )(*queries, *keys, *values, image_gain, text_gain, usable)


def extended(block, sides, width):
    for axis, dim in sides:
        count = lax.axis_size(axis)
        forward = [(i, i + 1) for i in range(count - 1)]
        backward = [(target, source) for source, target in forward]
        low = lax.ppermute(
            lax.slice_in_dim(block, block.shape[dim] - width, None, axis=dim), axis, forward
        )
        high = lax.ppermute(lax.slice_in_dim(block, 0, width, axis=dim), axis, backward)
        block = jnp.concatenate([low, block, high], axis=dim)
    return block


def convolve(padded, kernel):
    out_rows = padded.shape[1] - 2
    out_cols = padded.shape[2] - 2
    patches = jnp.concatenate(
        [
            padded[:, row : row + out_rows, col : col + out_cols]
            for row in range(3)
            for col in range(3)
        ],
        -1,
    )
    flat = kernel.reshape(-1, kernel.shape[-1])
    return jnp.einsum(
        "rhwc,co->rhwo", patches, flat, preferred_element_type=jnp.float32
    ).astype(jnp.bfloat16)


def body(
    image_hidden,
    text_hidden,
    latent_grid,
    text_lengths,
    step_index,
    image_mod,
    text_mod,
    final_mod,
    image_qk_gain,
    text_qk_gain,
    image_qkv,
    text_qkv,
    image_proj,
    text_proj,
    image_up,
    text_up,
    image_down,
    text_down,
    final_proj,
    conv_kernel,
):
    heads, blocks = lax.axis_size("head"), lax.axis_size("blk")
    my_head, my_blk = lax.axis_index("head"), lax.axis_index("blk")
    requests, tile_rows, tile_cols, model = image_hidden.shape
    slots = text_hidden.shape[1]
    mine = requests // blocks
    patches = tile_rows * tile_cols

    def of_block(array, block):
        return lax.dynamic_slice_in_dim(array, block * mine, mine, axis=0)

    def scatter(array):
        pieces = [of_block(array, my_blk)]
        for off in range(1, blocks):
            perm = [(i, (i + off) % blocks) for i in range(blocks)]
            pieces.append(lax.ppermute(of_block(array, (my_blk + off) % blocks), "blk", perm))
        return pieces

    def collect(pieces):
        held = [pieces[0]]
        for off in range(1, blocks):
            perm = [(i, (i - off) % blocks) for i in range(blocks)]
            held.append(lax.ppermute(pieces[off], "blk", perm))
        placed = jnp.zeros((requests,) + held[0].shape[1:], held[0].dtype)
        for off, piece in enumerate(held):
            spot = ((my_blk + off) % blocks) * mine
            placed = lax.dynamic_update_slice_in_dim(placed, piece, spot, axis=0)
        return placed

    def fetch(array, off):
        return lax.ppermute(array, "head", [(i, (i - off) % heads) for i in range(heads)])

    def give(array, off):
        return lax.ppermute(array, "head", [(i, (i + off) % heads) for i in range(heads)])

    image_m, text_m, final_m = (of_block(a, my_blk) for a in (image_mod, text_mod, final_mod))
    lengths = of_block(text_lengths, my_blk)

    text_x = scatter(text_hidden)
    image_x = scatter(image_hidden.reshape(requests, patches, model))
    text_x = jnp.concatenate(text_x, 1).astype(jnp.float32)
    text_a = modulate(text_x, text_m[:, 0], text_m[:, 1]).astype(jnp.bfloat16)
    text_all = jnp.concatenate([text_a] + [fetch(text_a, off) for off in range(1, heads)], 1)
    image_a = []
    for index in range(blocks):
        if index:
            image_x[index], image_a[-1] = apart((image_x[index], image_a[-1]))
        piece = image_x[index].astype(jnp.float32)
        image_x[index] = piece
        image_a.append(
            apart(modulate(piece, image_m[:, 0], image_m[:, 1]).astype(jnp.bfloat16))
        )
    parts = [jnp.concatenate(image_a, 1)]
    for off in range(1, heads):
        parts.append(jnp.concatenate([fetch(piece, off) for piece in image_a], 1))

    position = jnp.arange(heads * blocks * slots, dtype=jnp.int32)
    head_off = position // (blocks * slots)
    blk_off = (position // slots) % blocks
    owner = ((my_head + head_off) % heads) * blocks + (my_blk - blk_off) % blocks
    slot_ids = owner * slots + position % slots
    usable = (slot_ids[None, :] < lengths[:, None]).astype(jnp.float32)[:, :, None]

    queries, keys, values = [], [], []
    for tokens, weight in [(part, image_qkv) for part in parts] + [(text_all, text_qkv)]:
        queries.append(dot(tokens, weight[:, 0]))
        keys.append(dot(tokens, weight[:, 1]))
        values.append(dot(tokens, weight[:, 2]).astype(jnp.bfloat16))
    attend_rest = functools.partial(
        attend,
        keys=keys,
        values=values,
        image_gain=image_qk_gain,
        text_gain=text_qk_gain,
        usable=usable,
    )
    per = blocks // CHUNKS
    spans = [slice(c * per * patches, (c + 1) * per * patches) for c in range(CHUNKS)]
    own_queries = [queries[0], queries[-1]]
    shares = [[] for _ in spans]
    if heads > 1:
        others = attend_rest(queries[1:-1], -1)
        for chunk, span in enumerate(spans):
            for other in others:
                shares[chunk].append(dot(other[:, span], image_proj).astype(jnp.bfloat16))
        own_queries, shares = apart((own_queries, shares))
    own_context, text_context = attend_rest(own_queries, 1)

    def gathered(own, shares):
        total = apart(own)
        for off, share in enumerate(shares, 1):
            total = total + give(share, off).astype(jnp.float32)
        return total

    def middle(hidden, mod, total):
        mid = hidden + mod[:, 2][:, None, :] * total
        return mid, apart(modulate(mid, mod[:, 3], mod[:, 4]).astype(jnp.bfloat16))

    def expanded(local, up, down):
        results = []
        for off in range(heads):
            tokens = fetch(local, off) if off else local
            hid = jax.nn.gelu(dot(tokens, up), approximate=True).astype(jnp.bfloat16)
            result = dot(hid, down)
            results.append(result.astype(jnp.bfloat16) if off else result)
        return gathered(results[0], results[1:])

    middles = []
    for chunk, span in enumerate(spans):
        total = gathered(dot(own_context[:, span], image_proj), shares[chunk])
        hidden = jnp.concatenate(image_x[chunk * per : (chunk + 1) * per], 1)
        middles.append(middle(hidden, image_m, total))

    width = blocks * slots
    text_shares = [
        dot(text_context[:, off * width : (off + 1) * width], text_proj) for off in range(heads)
    ]
    total = gathered(text_shares[0], [share.astype(jnp.bfloat16) for share in text_shares[1:]])
    text_mid, text_local = middle(text_x, text_m, total)
    text_y = text_mid + text_m[:, 5][:, None, :] * expanded(text_local, text_up, text_down)
    text_y = text_y.astype(jnp.bfloat16)

    state_pieces, velocity_pieces = [], []
    for mid, local in middles:
        image_y = mid + image_m[:, 5][:, None, :] * expanded(local, image_up, image_down)
        final_in = modulate(image_y, final_m[:, 1], final_m[:, 0]).astype(jnp.bfloat16)
        velocity = dot(final_in, final_proj)
        for piece in range(per):
            rows = slice(piece * patches, (piece + 1) * patches)
            velocity_pieces.append(velocity[:, rows])
            state_pieces.append(image_y[:, rows].astype(jnp.bfloat16))

    velocity = collect(velocity_pieces)
    image_states = collect(state_pieces).reshape(image_hidden.shape)
    text_states = collect([text_y[:, i * slots : (i + 1) * slots] for i in range(blocks)])

    channels = velocity.shape[-1] // 4
    velocity = (
        velocity.reshape(requests, tile_rows, tile_cols, 2, 2, channels)
        .transpose(0, 1, 3, 2, 4, 5)
        .reshape(requests, 2 * tile_rows, 2 * tile_cols, channels)
    )
    current = step_index.astype(jnp.float32) / 1000.0
    following = jnp.maximum(step_index - 125, 0).astype(jnp.float32) / 1000.0
    step_size = noise_level(following) - noise_level(current)
    latent_next = latent_grid + step_size[:, None, None, None] * velocity
    decoded_in = (latent_next / 1.5305 + 0.0609).astype(jnp.bfloat16)
    padded = extended(decoded_in, (("head", 1), ("blk", 2)), 1)
    features = convolve(padded, conv_kernel)
    return (image_states, text_states, latent_next, features)


def solution(mesh):
    in_specs = (
        P("req", "head", "blk", None),
        P("req", ("head", "blk"), None),
        P("req", "head", "blk", None),
        P("req"),
        P("req"),
        P("req", None, None),
        P("req", None, None),
        P("req", None, None),
        P(),
        P(),
        P(None, None, "head"),
        P(None, None, "head"),
        P("head", None),
        P("head", None),
        P(None, "head"),
        P(None, "head"),
        P("head", None),
        P("head", None),
        P(),
        P(),
    )
    out_specs = (
        P("req", "head", "blk", None),
        P("req", ("head", "blk"), None),
        P("req", "head", "blk", None),
        P("req", "head", "blk", None),
    )
    return jax.shard_map(body, mesh=mesh, in_specs=in_specs, out_specs=out_specs, check_vma=False)
```
